32 devices in a mesh: rows: 16 (over z, y, core), cols: 2 (over x).
Axes of the slice: x: 2, y: 2, z: 4, core: 2. Of those that a mesh axis runs over, the one named last changes fastest.
Arguments:
- elevation: float32 [512, 1024], P('rows', 'cols'), may hold values from -4.5 to 4.5
- water_depth: float32 [512, 1024], P('rows', 'cols'), may hold values from 1 to 40
- friction: float32 [512, 1024], P('rows', 'cols'), may hold values from 0.1 to 2
- current_x: float32 [512, 1024], P('rows', 'cols'), may hold values from -0.9 to 0.9
- wet_mask: int32 [512, 1024], P('rows', 'cols'), may hold values from 0 to 1, as said below
Outputs:
- new_elevation: float32 [512, 1024], P('rows', 'cols')
The draws below stay inside these ranges and needn't reach their ends.
Inputs may be any that keep to these rules, and one draw needn't show every extreme that they name: `wet_mask`: 1 marks a wet cell, 0 a dry one.
All inputs are finite; a program needn't handle non-finite values.
Results may differ from the reference program's by a relative error of at most 0.0003.
Values sent between devices are 32-bit elements; how exact they have to be, the bound alone decides.
A program may use at most 64 MiB of HBM per device.

```python
import math
import jax
import jax.numpy as jnp
from jax import lax

NY = 512
NX = 1024


def draw_elevation(key, part):
    key = jax.random.fold_in(key, 11)
    phase_key, rough_key = jax.random.split(key)
    phases = jax.random.uniform(phase_key, (3,), jnp.float32, 0.0, 2.0 * math.pi)
    north = (jnp.arange(NY, dtype=jnp.float32) / NY)[:, None]
    east = (jnp.arange(NX, dtype=jnp.float32) / NX)[None, :]
    smooth = jnp.cos(2.0 * math.pi * north + phases[0]) * jnp.cos(4.0 * math.pi * east + phases[1])
    smooth = smooth + 0.5 * jnp.cos(2.0 * math.pi * (3.0 * north + east) + phases[2])
    rough = 0.7 * jnp.clip(jax.random.normal(rough_key, (NY, NX), jnp.float32), -4.0, 4.0)
    return smooth + rough


def draw_wet_mask(key, part):
    key = jax.random.fold_in(key, 23)
    coast_key, top_key, left_key, height_key, width_key = jax.random.split(key, 5)
    coast = jax.random.randint(coast_key, (NY,), 0, NX // 2 + 1)
    north = jnp.arange(NY)
    east = jnp.arange(NX)
    dry_cells = east[None, :] < coast[:, None]
    top_rows = jax.random.randint(top_key, (16,), 0, NY)
    left_cols = jax.random.randint(left_key, (16,), NX // 4, NX)
    heights = jax.random.randint(height_key, (16,), 1, max(2, NY // 16))
    widths = jax.random.randint(width_key, (16,), 1, max(2, NX // 16))
    for island in range(16):
        rows_inside = (north >= top_rows[island]) & (north < top_rows[island] + heights[island])
        cols_inside = (east >= left_cols[island]) & (east < left_cols[island] + widths[island])
        dry_cells = dry_cells | rows_inside[:, None] & cols_inside[None, :]
    return jnp.where(dry_cells, 0, 1).astype(jnp.int32)


def levels(rng, shape, shards, low, largest):
    factor_of, own = 1.0, jax.random.fold_in(rng, 6)
    for axis_at, blocks in shards:
        steps = jnp.exp(jax.random.uniform(jax.random.fold_in(own, axis_at), (blocks,), jnp.float32, low / len(shards), largest / len(shards)))
        factor_of = factor_of * jnp.repeat(steps, shape[axis_at] // blocks).reshape([-1 if axis == axis_at else 1 for axis in range(len(shape))])
    return factor_of


def setup_inputs(seed: int = 0) -> dict:
    key_of = jax.random.split(jax.random.key(seed), 6)
    elevation = draw_elevation(jax.random.fold_in(key_of[5], 71), 0)
    water_depth = jnp.clip(jnp.exp(math.log(40.0) - 3.6888795 * jax.random.uniform(key_of[1], (NY, NX), jnp.float32) ** levels(key_of[1], (NY, NX), ((0, 16), (1, 2)), -0.2, 0.2)), 1.0, 40.0)
    friction = jnp.clip(jnp.exp(math.log(2.0) - 2.9957323 * jax.random.uniform(key_of[2], (NY, NX), jnp.float32) ** levels(key_of[2], (NY, NX), ((0, 16), (1, 2)), -0.2, 0.2)), 0.1, 2.0)
    current_x = jnp.clip(jax.random.uniform(key_of[3], (NY, NX), jnp.float32, -0.9, 0.9) * levels(key_of[3], (NY, NX), ((0, 16), (1, 2)), -0.4, 0.0), -0.9, 0.9)
    wet_mask = draw_wet_mask(jax.random.fold_in(key_of[5], 71), 0)
    return {"elevation": elevation, "water_depth": water_depth, "friction": friction, "current_x": current_x, "wet_mask": wet_mask}


coupling = 100.0

def face_weights(wet_depth):
    interior = coupling * jnp.sqrt(wet_depth[:, :-1] * wet_depth[:, 1:])
    return jnp.concatenate([interior, jnp.zeros_like(wet_depth[:, :1])], axis=1)

def advect(values, courant):
    padded = jnp.pad(values, ((0, 0), (1, 1)))
    forward = padded[:, 2:]
    backward = padded[:, :-2]
    return 0.5 * courant * (forward - backward) - 0.5 * courant * courant * (forward - 2.0 * values + backward)

def implicit_solve(couplings, damping, right_side):
    left_faces = jnp.concatenate([jnp.zeros_like(couplings[:, :1]), couplings[:, :-1]], axis=1)
    sub_diag = -0.5 * left_faces
    super_diag = -0.5 * couplings
    middle = 1.0 + damping + 0.5 * (left_faces + couplings)
    solved = lax.linalg.tridiagonal_solve(sub_diag, middle, super_diag, right_side[..., None])
    return solved[..., 0]

def reference(elevation, water_depth, friction, current_x, wet_mask):
    wet_depth = water_depth * wet_mask.astype(jnp.float32)
    damping = friction / (4.0 * water_depth)
    faces_x = face_weights(wet_depth)
    faces_y = face_weights(wet_depth.T)
    first_rhs = (1.0 - damping) * elevation
    half_step = implicit_solve(faces_x, damping, first_rhs)
    second_rhs = (1.0 - damping) * half_step - advect(half_step, current_x)
    new_elevation = implicit_solve(faces_y, damping.T, second_rhs.T).T
    return new_elevation
```

```python
import functools

import jax
import jax.numpy as jnp
from jax import lax
from jax.experimental import pallas as pl
from jax.experimental.pallas import tpu as pltpu
from jax.sharding import PartitionSpec as P

half_coupling = 50.0
LANES = 128


def rolled(values, shift, axis):
    return pltpu.roll(values, shift % values.shape[axis], axis)


def reduce_lines(face, excess, rights, axis):
    length = face.shape[axis]
    before = rolled(face, 1, axis)
    stride = 1
    while stride < length:
        inverse = 1.0 / (excess + before + face)
        to_next = face * inverse
        to_prev = before * inverse
        through = to_next * before
        excess = (
            excess
            + rolled(to_next * excess, stride, axis)
            + rolled(to_prev * excess, -stride, axis)
        )
        rights = [
            right
            + rolled(to_next * right, stride, axis)
            + rolled(to_prev * right, -stride, axis)
            for right in rights
        ]
        face = rolled(through, -stride, axis)
        before = rolled(through, stride, axis)
        stride *= 2
    inverse = 1.0 / excess
    return [right * inverse for right in rights]


def reduce_fluxes(lower, middle, upper, rights):
    count = len(middle)
    stride = 1
    while stride < count:
        inverse = [1.0 / m for m in middle]
        new_lower, new_middle, new_upper = [], [], []
        new_rights = [[] for _ in rights]
        for k in range(count):
            a, c, m = None, None, middle[k]
            sums = [right[k] for right in rights]
            if k - stride >= 0:
                w = lower[k] * inverse[k - stride]
                if k - 2 * stride >= 0:
                    a = w * lower[k - stride]
                m = m - w * upper[k - stride]
                sums = [s + w * right[k - stride] for s, right in zip(sums, rights)]
            if k + stride < count:
                w = upper[k] * inverse[k + stride]
                if k + 2 * stride < count:
                    c = w * upper[k + stride]
                m = m - w * lower[k + stride]
                sums = [s + w * right[k + stride] for s, right in zip(sums, rights)]
            new_lower.append(a)
            new_middle.append(m)
            new_upper.append(c)
            for out, s in zip(new_rights, sums):
                out.append(s)
        lower, middle, upper, rights = new_lower, new_middle, new_upper, new_rights
        stride *= 2
    inverse = [1.0 / m for m in middle]
    return [[s * i for s, i in zip(right, inverse)] for right in rights]


def flux_system(weights, first_first, last_first, last_last):
    count = len(weights)
    lower = [weights[k] * last_first[k] for k in range(count)]
    upper = [weights[k] * last_first[k + 1] for k in range(count)]
    middle = [1.0 + weights[k] * (last_last[k] + first_first[k + 1]) for k in range(count)]
    return lower, middle, upper


def step_kernel(
    nr, nc, elevation, depth, friction, current, mask, out,
    xbuf, kbuf, pbuf, x_send, x_recv, k_send, k_recv, p_send, p_recv,
):
    row_at, col_at = lax.axis_index("rows"), lax.axis_index("cols")
    height, width = out.shape
    chunks = width // LANES

    def row_peer(offset):
        return (lax.rem(row_at + offset, nr), col_at)

    def col_peer(offset):
        return (row_at, lax.rem(col_at + offset, nc))

    def row_copies(buffer, send, recv):
        return [
            pltpu.make_async_remote_copy(
                src_ref=buffer.at[row_at], dst_ref=buffer.at[row_at],
                send_sem=send.at[k - 1], recv_sem=recv.at[k - 1],
                device_id=row_peer(k), device_id_type=pl.DeviceIdType.MESH,
            )
            for k in range(1, nr)
        ]

    barrier = pltpu.get_barrier_semaphore()
    for k in range(1, nr):
        pl.semaphore_signal(barrier, inc=1, device_id=row_peer(k), device_id_type=pl.DeviceIdType.MESH)
    for k in range(1, nc):
        pl.semaphore_signal(barrier, inc=1, device_id=col_peer(k), device_id_type=pl.DeviceIdType.MESH)

    still = depth[...]
    wet = still * mask[...].astype(jnp.float32)
    damping = friction[...] / (4.0 * still)
    excess = 1.0 + damping
    lane = lax.broadcasted_iota(jnp.int32, (height, width), 1)
    row = lax.broadcasted_iota(jnp.int32, (height, width), 0)

    face = half_coupling * jnp.sqrt(wet * rolled(wet, -1, 0))
    face = jnp.where(row == height - 1, 0.0, face)
    unit_first = jnp.where(row == 0, 1.0, 0.0)
    unit_last = jnp.where(row == height - 1, 1.0, 0.0)
    from_first, from_last = reduce_lines(face, excess, [unit_first, unit_last], 0)
    ends = (
        from_first[0:1], from_first[height - 1 : height], from_last[height - 1 : height],
        wet[0:1], wet[height - 1 : height],
    )
    for q, line in enumerate(ends):
        for c in range(chunks):
            kbuf[row_at, q, c : c + 1, :] = line[:, c * LANES : (c + 1) * LANES]

    pl.semaphore_wait(barrier, nr + nc - 2)
    k_copies = row_copies(kbuf, k_send, k_recv)
    for copy in k_copies:
        copy.start()

    face_x = half_coupling * jnp.sqrt(wet * rolled(wet, -1, 1))
    face_x = jnp.where(lane == width - 1, 0.0, face_x)
    first_rhs = (1.0 - damping) * elevation[...]
    small = lax.broadcasted_iota(jnp.int32, (height, LANES), 1)
    at_left = col_at == 0
    if nc == 2:
        edge = jnp.where(at_left, width - 1, 0)
        unit = jnp.where(lane == edge, 1.0, 0.0)
        solved, spike = reduce_lines(face_x, excess, [first_rhs, unit], 1)
        message = None
        for q, values in enumerate((solved, spike, wet)):
            chunk = jnp.where(at_left, values[:, width - LANES :], values[:, :LANES])
            chunk = pltpu.roll(chunk, q + jnp.where(at_left, 1, 0), 1)
            message = chunk if q == 0 else jnp.where(small == q, chunk, message)
    else:
        units = [jnp.where(lane == 0, 1.0, 0.0), jnp.where(lane == width - 1, 1.0, 0.0)]
        solved, from_left, from_right = reduce_lines(face_x, excess, [first_rhs] + units, 1)
        message = jnp.zeros((height, LANES), jnp.float32)
        columns = (
            solved[:, 0:1], solved[:, width - 1 : width], from_left[:, 0:1],
            from_left[:, width - 1 : width], from_right[:, width - 1 : width],
            wet[:, 0:1], wet[:, width - 1 : width],
        )
        for q, column in enumerate(columns):
            message = jnp.where(small == q, column, message)
    xbuf[col_at] = message
    x_copies = [
        pltpu.make_async_remote_copy(
            src_ref=xbuf.at[col_at], dst_ref=xbuf.at[col_at],
            send_sem=x_send.at[k - 1], recv_sem=x_recv.at[k - 1],
            device_id=col_peer(k), device_id_type=pl.DeviceIdType.MESH,
        )
        for k in range(1, nc)
    ]
    for copy in x_copies:
        copy.start()
    for copy in x_copies:
        copy.wait_recv()

    if nc == 2:
        other = xbuf[1 - col_at]
        p, s, w = (message[:, q : q + 1] for q in range(3))
        other_p, other_s, other_w = (other[:, q : q + 1] for q in range(3))
        weight = half_coupling * jnp.sqrt(w * other_w)
        flux = weight * (p - other_p) / (1.0 + weight * (s + other_s))
        half_step = solved - spike * flux
        beyond = other_p + other_s * flux
        right_of = jnp.where(at_left, beyond, 0.0)
        left_of = jnp.where(at_left, 0.0, beyond)
    else:
        got = [xbuf[k] for k in range(nc)]
        pf, pb, ff, fl, ll, wf, wl = ([g[:, q : q + 1] for g in got] for q in range(7))
        weights = [half_coupling * jnp.sqrt(wl[k] * wf[k + 1]) for k in range(nc - 1)]
        system = flux_system(weights, ff, fl, ll)
        (fluxes,) = reduce_fluxes(
            *system, [[weights[k] * (pb[k] - pf[k + 1]) for k in range(nc - 1)]]
        )
        zero = jnp.zeros_like(fluxes[0])
        fluxes = [zero] + fluxes + [zero]
        first = [pf[k] + ff[k] * fluxes[k] - fl[k] * fluxes[k + 1] for k in range(nc)] + [zero]
        last = [zero] + [pb[k] + fl[k] * fluxes[k] - ll[k] * fluxes[k + 1] for k in range(nc)]
        entering, leaving, left_of, right_of = zero, zero, zero, zero
        for k in range(nc):
            here = col_at == k
            entering = jnp.where(here, fluxes[k], entering)
            leaving = jnp.where(here, fluxes[k + 1], leaving)
            left_of = jnp.where(here, last[k], left_of)
            right_of = jnp.where(here, first[k + 1], right_of)
        half_step = solved + from_left * entering - from_right * leaving

    courant = current[...]
    forward = jnp.where(lane == width - 1, right_of, rolled(half_step, -1, 1))
    backward = jnp.where(lane == 0, left_of, rolled(half_step, 1, 1))
    advected = 0.5 * courant * (forward - backward) - 0.5 * courant * courant * (
        forward - 2.0 * half_step + backward
    )
    second_rhs = (1.0 - damping) * half_step - advected

    for q, response in enumerate((from_first, from_last)):
        line = jnp.sum(response * second_rhs, axis=0, keepdims=True)
        for c in range(chunks):
            pbuf[row_at, q, c : c + 1, :] = line[:, c * LANES : (c + 1) * LANES]
    p_copies = row_copies(pbuf, p_send, p_recv)
    for copy in p_copies:
        copy.start()

    (solved_y,) = reduce_lines(face, excess, [second_rhs], 0)

    for copy in k_copies:
        copy.wait_recv()
    ff, fl, ll, wf, wl = ([kbuf[k, q] for k in range(nr)] for q in range(5))
    weights = [half_coupling * jnp.sqrt(wl[k] * wf[k + 1]) for k in range(nr - 1)]
    system = flux_system(weights, ff, fl, ll)
    rights = [
        [jnp.where(row_at + shift == k, weights[k], 0.0) for k in range(nr - 1)]
        for shift in (-1, 0)
    ]
    into, outof = reduce_fluxes(*system, rights)

    for copy in p_copies:
        copy.wait_recv()
    entering = leaving = jnp.zeros((chunks, LANES), jnp.float32)
    for k in range(nr - 1):
        jump = pbuf[k, 1] - pbuf[k + 1, 0]
        entering = entering + into[k] * jump
        leaving = leaving + outof[k] * jump
    for c in range(chunks):
        at = slice(c * LANES, (c + 1) * LANES)
        out[:, at] = (
            solved_y[:, at]
            + from_first[:, at] * entering[c : c + 1, :]
            - from_last[:, at] * leaving[c : c + 1, :]
        )

    for copy in k_copies + x_copies + p_copies:
        copy.wait_send()


def on_device(elevation, water_depth, friction, current_x, wet_mask):
    nr, nc = lax.axis_size("rows"), lax.axis_size("cols")
    height, width = elevation.shape
    chunks = width // LANES
    return pl.pallas_call(
        functools.partial(step_kernel, nr, nc),
        out_shape=jax.ShapeDtypeStruct(elevation.shape, jnp.float32),
        in_specs=[pl.BlockSpec(memory_space=pltpu.VMEM)] * 5,
        out_specs=pl.BlockSpec(memory_space=pltpu.VMEM),
        scratch_shapes=[
            pltpu.VMEM((nc, height, LANES), jnp.float32),
            pltpu.VMEM((nr, 5, chunks, LANES), jnp.float32),
            pltpu.VMEM((nr, 2, chunks, LANES), jnp.float32),
            pltpu.SemaphoreType.DMA((nc - 1,)),
            pltpu.SemaphoreType.DMA((nc - 1,)),
            pltpu.SemaphoreType.DMA((nr - 1,)),
            pltpu.SemaphoreType.DMA((nr - 1,)),
            pltpu.SemaphoreType.DMA((nr - 1,)),
            pltpu.SemaphoreType.DMA((nr - 1,)),
        ],
        compiler_params=pltpu.CompilerParams(
            collective_id=0, has_side_effects=True, vmem_limit_bytes=32 * 1024 * 1024
        ),
    )(elevation, water_depth, friction, current_x, wet_mask)


def solution(mesh):
    placed = P("rows", "cols")
    return jax.shard_map(
        on_device, mesh=mesh, in_specs=(placed,) * 5, out_specs=placed, check_vma=False
    )
```

```python
import functools

import jax
import jax.numpy as jnp
from jax import lax
from jax.experimental import pallas as pl
from jax.experimental.pallas import tpu as pltpu
from jax.sharding import PartitionSpec as P

half_coupling = 50.0
LANES = 128


def rolled(values, shift, axis):
    return pltpu.roll(values, shift % values.shape[axis], axis)


def reduce_lines(face, excess, rights, axis):
    length = face.shape[axis]
    before = rolled(face, 1, axis)
    stride = 1
    while stride < length:
        inverse = 1.0 / (excess + before + face)
        to_next = face * inverse
        to_prev = before * inverse
        through = to_next * before
        excess = (
            excess
            + rolled(to_next * excess, stride, axis)
            + rolled(to_prev * excess, -stride, axis)
        )
        rights = [
            right
            + rolled(to_next * right, stride, axis)
            + rolled(to_prev * right, -stride, axis)
            for right in rights
        ]
        face = rolled(through, -stride, axis)
        before = rolled(through, stride, axis)
        stride *= 2
    inverse = 1.0 / excess
    return [right * inverse for right in rights]


def reduce_fluxes(lower, middle, upper, rights):
    count = len(middle)
    stride = 1
    while stride < count:
        inverse = [1.0 / m for m in middle]
        new_lower, new_middle, new_upper = [], [], []
        new_rights = [[] for _ in rights]
        for k in range(count):
            a, c, m = None, None, middle[k]
            sums = [right[k] for right in rights]
            if k - stride >= 0:
                w = lower[k] * inverse[k - stride]
                if k - 2 * stride >= 0:
                    a = w * lower[k - stride]
                m = m - w * upper[k - stride]
                sums = [s + w * right[k - stride] for s, right in zip(sums, rights)]
            if k + stride < count:
                w = upper[k] * inverse[k + stride]
                if k + 2 * stride < count:
                    c = w * upper[k + stride]
                m = m - w * lower[k + stride]
                sums = [s + w * right[k + stride] for s, right in zip(sums, rights)]
            new_lower.append(a)
            new_middle.append(m)
            new_upper.append(c)
            for out, s in zip(new_rights, sums):
                out.append(s)
        lower, middle, upper, rights = new_lower, new_middle, new_upper, new_rights
        stride *= 2
    inverse = [1.0 / m for m in middle]
    return [[s * i for s, i in zip(right, inverse)] for right in rights]


def flux_system(weights, first_first, last_first, last_last):
    count = len(weights)
    lower = [weights[k] * last_first[k] for k in range(count)]
    upper = [weights[k] * last_first[k + 1] for k in range(count)]
    middle = [1.0 + weights[k] * (last_last[k] + first_first[k + 1]) for k in range(count)]
    return lower, middle, upper


def step_kernel(
    nr, nc, elevation_hbm, depth_hbm, friction_hbm, current_hbm, mask_hbm, out,
    elevation, depth, friction, current, mask, in_sem,
    xbuf, kbuf, pbuf, x_send, x_recv, k_send, k_recv, p_send, p_recv,
):
    row_at, col_at = lax.axis_index("rows"), lax.axis_index("cols")
    height, width = out.shape
    chunks = width // LANES

    def row_peer(offset):
        return (lax.rem(row_at + offset, nr), col_at)

    def col_peer(offset):
        return (row_at, lax.rem(col_at + offset, nc))

    def row_copies(buffer, send, recv):
        return [
            pltpu.make_async_remote_copy(
                src_ref=buffer.at[row_at], dst_ref=buffer.at[row_at],
                send_sem=send.at[k - 1], recv_sem=recv.at[k - 1],
                device_id=row_peer(k), device_id_type=pl.DeviceIdType.MESH,
            )
            for k in range(1, nr)
        ]

    barrier = pltpu.get_barrier_semaphore()
    for k in range(1, nr):
        pl.semaphore_signal(barrier, inc=1, device_id=row_peer(k), device_id_type=pl.DeviceIdType.MESH)
    for k in range(1, nc):
        pl.semaphore_signal(barrier, inc=1, device_id=col_peer(k), device_id_type=pl.DeviceIdType.MESH)

    arrays = (
        (depth_hbm, depth), (mask_hbm, mask), (friction_hbm, friction),
        (elevation_hbm, elevation), (current_hbm, current),
    )
    loads = [
        pltpu.make_async_copy(src, dst, in_sem.at[i]) for i, (src, dst) in enumerate(arrays)
    ]
    for load in loads:
        load.start()

    for load in loads[:3]:
        load.wait()
    still = depth[...]
    wet = still * mask[...].astype(jnp.float32)
    damping = friction[...] / (4.0 * still)
    excess = 1.0 + damping
    lane = lax.broadcasted_iota(jnp.int32, (height, width), 1)
    row = lax.broadcasted_iota(jnp.int32, (height, width), 0)

    face_x = half_coupling * jnp.sqrt(wet * rolled(wet, -1, 1))
    face_x = jnp.where(lane == width - 1, 0.0, face_x)
    loads[3].wait()
    first_rhs = (1.0 - damping) * elevation[...]
    small = lax.broadcasted_iota(jnp.int32, (height, LANES), 1)
    at_left = col_at == 0
    if nc == 2:
        edge = jnp.where(at_left, width - 1, 0)
        unit = jnp.where(lane == edge, 1.0, 0.0)
        solved, spike = reduce_lines(face_x, excess, [first_rhs, unit], 1)
        message = None
        for q, values in enumerate((solved, spike, wet)):
            chunk = jnp.where(at_left, values[:, width - LANES :], values[:, :LANES])
            chunk = pltpu.roll(chunk, q + jnp.where(at_left, 1, 0), 1)
            message = chunk if q == 0 else jnp.where(small == q, chunk, message)
    else:
        units = [jnp.where(lane == 0, 1.0, 0.0), jnp.where(lane == width - 1, 1.0, 0.0)]
        solved, from_left, from_right = reduce_lines(face_x, excess, [first_rhs] + units, 1)
        message = jnp.zeros((height, LANES), jnp.float32)
        columns = (
            solved[:, 0:1], solved[:, width - 1 : width], from_left[:, 0:1],
            from_left[:, width - 1 : width], from_right[:, width - 1 : width],
            wet[:, 0:1], wet[:, width - 1 : width],
        )
        for q, column in enumerate(columns):
            message = jnp.where(small == q, column, message)
    xbuf[col_at] = message
    x_copies = [
        pltpu.make_async_remote_copy(
            src_ref=xbuf.at[col_at], dst_ref=xbuf.at[col_at],
            send_sem=x_send.at[k - 1], recv_sem=x_recv.at[k - 1],
            device_id=col_peer(k), device_id_type=pl.DeviceIdType.MESH,
        )
        for k in range(1, nc)
    ]
    pl.semaphore_wait(barrier, nr + nc - 2)
    for copy in x_copies:
        copy.start()

    face = half_coupling * jnp.sqrt(wet * rolled(wet, -1, 0))
    face = jnp.where(row == height - 1, 0.0, face)
    unit_first = jnp.where(row == 0, 1.0, 0.0)
    unit_last = jnp.where(row == height - 1, 1.0, 0.0)
    from_first, from_last = reduce_lines(face, excess, [unit_first, unit_last], 0)
    ends = (
        from_first[0:1], from_first[height - 1 : height], from_last[height - 1 : height],
        wet[0:1], wet[height - 1 : height],
    )
    for q, line in enumerate(ends):
        for c in range(chunks):
            kbuf[row_at, q, c : c + 1, :] = line[:, c * LANES : (c + 1) * LANES]
    k_copies = row_copies(kbuf, k_send, k_recv)
    for copy in k_copies:
        copy.start()

    for copy in x_copies:
        copy.wait_recv()

    if nc == 2:
        other = xbuf[1 - col_at]
        p, s, w = (message[:, q : q + 1] for q in range(3))
        other_p, other_s, other_w = (other[:, q : q + 1] for q in range(3))
        weight = half_coupling * jnp.sqrt(w * other_w)
        flux = weight * (p - other_p) / (1.0 + weight * (s + other_s))
        half_step = solved - spike * flux
        beyond = other_p + other_s * flux
        right_of = jnp.where(at_left, beyond, 0.0)
        left_of = jnp.where(at_left, 0.0, beyond)
    else:
        got = [xbuf[k] for k in range(nc)]
        pf, pb, ff, fl, ll, wf, wl = ([g[:, q : q + 1] for g in got] for q in range(7))
        weights = [half_coupling * jnp.sqrt(wl[k] * wf[k + 1]) for k in range(nc - 1)]
        system = flux_system(weights, ff, fl, ll)
        (fluxes,) = reduce_fluxes(
            *system, [[weights[k] * (pb[k] - pf[k + 1]) for k in range(nc - 1)]]
        )
        zero = jnp.zeros_like(fluxes[0])
        fluxes = [zero] + fluxes + [zero]
        first = [pf[k] + ff[k] * fluxes[k] - fl[k] * fluxes[k + 1] for k in range(nc)] + [zero]
        last = [zero] + [pb[k] + fl[k] * fluxes[k] - ll[k] * fluxes[k + 1] for k in range(nc)]
        entering, leaving, left_of, right_of = zero, zero, zero, zero
        for k in range(nc):
            here = col_at == k
            entering = jnp.where(here, fluxes[k], entering)
            leaving = jnp.where(here, fluxes[k + 1], leaving)
            left_of = jnp.where(here, last[k], left_of)
            right_of = jnp.where(here, first[k + 1], right_of)
        half_step = solved + from_left * entering - from_right * leaving

    loads[4].wait()
    courant = current[...]
    forward = jnp.where(lane == width - 1, right_of, rolled(half_step, -1, 1))
    backward = jnp.where(lane == 0, left_of, rolled(half_step, 1, 1))
    advected = 0.5 * courant * (forward - backward) - 0.5 * courant * courant * (
        forward - 2.0 * half_step + backward
    )
    second_rhs = (1.0 - damping) * half_step - advected

    for q, response in enumerate((from_first, from_last)):
        line = jnp.sum(response * second_rhs, axis=0, keepdims=True)
        for c in range(chunks):
            pbuf[row_at, q, c : c + 1, :] = line[:, c * LANES : (c + 1) * LANES]
    p_copies = row_copies(pbuf, p_send, p_recv)
    for copy in p_copies:
        copy.start()

    (solved_y,) = reduce_lines(face, excess, [second_rhs], 0)

    for copy in k_copies:
        copy.wait_recv()
    ff, fl, ll, wf, wl = ([kbuf[k, q] for k in range(nr)] for q in range(5))
    weights = [half_coupling * jnp.sqrt(wl[k] * wf[k + 1]) for k in range(nr - 1)]
    system = flux_system(weights, ff, fl, ll)
    rights = [
        [jnp.where(row_at + shift == k, weights[k], 0.0) for k in range(nr - 1)]
        for shift in (-1, 0)
    ]
    into, outof = reduce_fluxes(*system, rights)

    for copy in p_copies:
        copy.wait_recv()
    entering = leaving = jnp.zeros((chunks, LANES), jnp.float32)
    for k in range(nr - 1):
        jump = pbuf[k, 1] - pbuf[k + 1, 0]
        entering = entering + into[k] * jump
        leaving = leaving + outof[k] * jump
    for c in range(chunks):
        at = slice(c * LANES, (c + 1) * LANES)
        out[:, at] = (
            solved_y[:, at]
            + from_first[:, at] * entering[c : c + 1, :]
            - from_last[:, at] * leaving[c : c + 1, :]
        )

    for copy in k_copies + x_copies + p_copies:
        copy.wait_send()


def on_device(elevation, water_depth, friction, current_x, wet_mask):
    nr, nc = lax.axis_size("rows"), lax.axis_size("cols")
    height, width = elevation.shape
    chunks = width // LANES
    return pl.pallas_call(
        functools.partial(step_kernel, nr, nc),
        out_shape=jax.ShapeDtypeStruct(elevation.shape, jnp.float32),
        in_specs=[pl.BlockSpec(memory_space=pl.ANY)] * 5,
        out_specs=pl.BlockSpec(memory_space=pltpu.VMEM),
        scratch_shapes=[pltpu.VMEM(elevation.shape, jnp.float32)] * 4
        + [
            pltpu.VMEM(elevation.shape, jnp.int32),
            pltpu.SemaphoreType.DMA((5,)),
            pltpu.VMEM((nc, height, LANES), jnp.float32),
            pltpu.VMEM((nr, 5, chunks, LANES), jnp.float32),
            pltpu.VMEM((nr, 2, chunks, LANES), jnp.float32),
            pltpu.SemaphoreType.DMA((nc - 1,)),
            pltpu.SemaphoreType.DMA((nc - 1,)),
            pltpu.SemaphoreType.DMA((nr - 1,)),
            pltpu.SemaphoreType.DMA((nr - 1,)),
            pltpu.SemaphoreType.DMA((nr - 1,)),
            pltpu.SemaphoreType.DMA((nr - 1,)),
        ],
        compiler_params=pltpu.CompilerParams(
            collective_id=0, has_side_effects=True, vmem_limit_bytes=60 * 1024 * 1024
        ),
    )(elevation, water_depth, friction, current_x, wet_mask)


def solution(mesh):
    placed = P("rows", "cols")
    return jax.shard_map(
        on_device, mesh=mesh, in_specs=(placed,) * 5, out_specs=placed, check_vma=False
    )
```

```python
import functools

import jax
import jax.numpy as jnp
from jax import lax
from jax.experimental import pallas as pl
from jax.experimental.pallas import tpu as pltpu
from jax.sharding import PartitionSpec as P

half_coupling = 50.0
LANES = 128


def rolled(values, shift, axis):
    return pltpu.roll(values, shift % values.shape[axis], axis)


def reduce_lines(face, excess, rights, axis):
    length = face.shape[axis]
    before = rolled(face, 1, axis)
    stride = 1
    steps = []

    def advance(right, to_next, to_prev, stride):
        return (
            right
            + rolled(to_next * right, stride, axis)
            + rolled(to_prev * right, -stride, axis)
        )

    while stride < length:
        inverse = 1.0 / (excess + before + face)
        to_next = face * inverse
        to_prev = before * inverse
        through = to_next * before
        excess = advance(excess, to_next, to_prev, stride)
        rights = [advance(right, to_next, to_prev, stride) for right in rights]
        steps.append((to_next, to_prev, stride))
        face = rolled(through, -stride, axis)
        before = rolled(through, stride, axis)
        stride *= 2
    inverse = 1.0 / excess

    def solve(right):
        for step in steps:
            right = advance(right, *step)
        return right * inverse

    return [right * inverse for right in rights], solve


def reduce_fluxes(lower, middle, upper, rights):
    count = len(middle)
    stride = 1
    while stride < count:
        inverse = [1.0 / m for m in middle]
        new_lower, new_middle, new_upper = [], [], []
        new_rights = [[] for _ in rights]
        for k in range(count):
            a, c, m = None, None, middle[k]
            sums = [right[k] for right in rights]
            if k - stride >= 0:
                w = lower[k] * inverse[k - stride]
                if k - 2 * stride >= 0:
                    a = w * lower[k - stride]
                m = m - w * upper[k - stride]
                sums = [s + w * right[k - stride] for s, right in zip(sums, rights)]
            if k + stride < count:
                w = upper[k] * inverse[k + stride]
                if k + 2 * stride < count:
                    c = w * upper[k + stride]
                m = m - w * lower[k + stride]
                sums = [s + w * right[k + stride] for s, right in zip(sums, rights)]
            new_lower.append(a)
            new_middle.append(m)
            new_upper.append(c)
            for out, s in zip(new_rights, sums):
                out.append(s)
        lower, middle, upper, rights = new_lower, new_middle, new_upper, new_rights
        stride *= 2
    inverse = [1.0 / m for m in middle]
    return [[s * i for s, i in zip(right, inverse)] for right in rights]


def flux_system(weights, first_first, last_first, last_last):
    count = len(weights)
    lower = [weights[k] * last_first[k] for k in range(count)]
    upper = [weights[k] * last_first[k + 1] for k in range(count)]
    middle = [1.0 + weights[k] * (last_last[k] + first_first[k + 1]) for k in range(count)]
    return lower, middle, upper


def step_kernel(
    nr, nc, elevation_hbm, depth_hbm, friction_hbm, current_hbm, mask_hbm, out,
    elevation, depth, friction, current, mask, in_sem,
    xbuf, kbuf, pbuf, x_send, x_recv, k_send, k_recv, p_send, p_recv,
):
    row_at, col_at = lax.axis_index("rows"), lax.axis_index("cols")
    height, width = out.shape
    chunks = width // LANES

    def row_peer(offset):
        return (lax.rem(row_at + offset, nr), col_at)

    def col_peer(offset):
        return (row_at, lax.rem(col_at + offset, nc))

    def send_rows(buffer, send, recv):
        for k in range(nr - 1):
            peer = jnp.where(k >= row_at, k + 1, k)
            pltpu.make_async_remote_copy(
                src_ref=buffer.at[row_at], dst_ref=buffer.at[row_at],
                send_sem=send, recv_sem=recv,
                device_id=(peer, col_at), device_id_type=pl.DeviceIdType.MESH,
            ).start()

    def wait_rows(buffer, semaphore):
        part = buffer.at[pl.ds(0, nr - 1)]
        pltpu.make_async_copy(part, part, semaphore).wait()

    arrays = (
        (depth_hbm, depth), (mask_hbm, mask), (friction_hbm, friction),
        (elevation_hbm, elevation), (current_hbm, current),
    )
    loads = [
        pltpu.make_async_copy(src, dst, in_sem.at[i]) for i, (src, dst) in enumerate(arrays)
    ]
    for load in loads:
        load.start()

    barrier = pltpu.get_barrier_semaphore()
    for k in range(1, nr):
        pl.semaphore_signal(barrier, inc=1, device_id=row_peer(k), device_id_type=pl.DeviceIdType.MESH)
    for k in range(1, nc):
        pl.semaphore_signal(barrier, inc=1, device_id=col_peer(k), device_id_type=pl.DeviceIdType.MESH)

    for load in loads[:3]:
        load.wait()
    still = depth[...]
    wet = still * mask[...].astype(jnp.float32)
    damping = friction[...] / (4.0 * still)
    excess = 1.0 + damping
    lane = lax.broadcasted_iota(jnp.int32, (height, width), 1)
    row = lax.broadcasted_iota(jnp.int32, (height, width), 0)

    face_x = half_coupling * jnp.sqrt(wet * rolled(wet, -1, 1))
    face_x = jnp.where(lane == width - 1, 0.0, face_x)
    loads[3].wait()
    first_rhs = (1.0 - damping) * elevation[...]
    small = lax.broadcasted_iota(jnp.int32, (height, LANES), 1)
    at_left = col_at == 0
    if nc == 2:
        edge = jnp.where(at_left, width - 1, 0)
        unit = jnp.where(lane == edge, 1.0, 0.0)
        (spike,), solve_x = reduce_lines(face_x, excess, [unit], 1)
        message = jnp.sum(spike * first_rhs, axis=1, keepdims=True)
        for q, values in ((1, spike), (2, wet)):
            chunk = jnp.where(at_left, values[:, width - LANES :], values[:, :LANES])
            chunk = pltpu.roll(chunk, q + jnp.where(at_left, 1, 0), 1)
            message = jnp.where(small == q, chunk, message)
    else:
        units = [jnp.where(lane == 0, 1.0, 0.0), jnp.where(lane == width - 1, 1.0, 0.0)]
        (from_left, from_right), solve_x = reduce_lines(face_x, excess, units, 1)
        solved = solve_x(first_rhs)
        message = jnp.zeros((height, LANES), jnp.float32)
        columns = (
            solved[:, 0:1], solved[:, width - 1 : width], from_left[:, 0:1],
            from_left[:, width - 1 : width], from_right[:, width - 1 : width],
            wet[:, 0:1], wet[:, width - 1 : width],
        )
        for q, column in enumerate(columns):
            message = jnp.where(small == q, column, message)
    xbuf[col_at] = message
    x_copies = [
        pltpu.make_async_remote_copy(
            src_ref=xbuf.at[col_at], dst_ref=xbuf.at[col_at],
            send_sem=x_send.at[k - 1], recv_sem=x_recv.at[k - 1],
            device_id=col_peer(k), device_id_type=pl.DeviceIdType.MESH,
        )
        for k in range(1, nc)
    ]
    pl.semaphore_wait(barrier, nr + nc - 2)
    for copy in x_copies:
        copy.start()

    face = half_coupling * jnp.sqrt(wet * rolled(wet, -1, 0))
    face = jnp.where(row == height - 1, 0.0, face)
    unit_first = jnp.where(row == 0, 1.0, 0.0)
    unit_last = jnp.where(row == height - 1, 1.0, 0.0)
    (from_first, from_last), solve_y = reduce_lines(face, excess, [unit_first, unit_last], 0)
    ends = (
        from_first[0:1], from_first[height - 1 : height], from_last[height - 1 : height],
        wet[0:1], wet[height - 1 : height],
    )
    for q, line in enumerate(ends):
        for c in range(chunks):
            kbuf[row_at, q, c : c + 1, :] = line[:, c * LANES : (c + 1) * LANES]
    send_rows(kbuf, k_send, k_recv)
    if nc == 2:
        solved = solve_x(first_rhs)

    for copy in x_copies:
        copy.wait_recv()

    if nc == 2:
        other = xbuf[1 - col_at]
        p, s, w = (message[:, q : q + 1] for q in range(3))
        other_p, other_s, other_w = (other[:, q : q + 1] for q in range(3))
        weight = half_coupling * jnp.sqrt(w * other_w)
        flux = weight * (p - other_p) / (1.0 + weight * (s + other_s))
        half_step = solved - spike * flux
        beyond = other_p + other_s * flux
        right_of = jnp.where(at_left, beyond, 0.0)
        left_of = jnp.where(at_left, 0.0, beyond)
    else:
        got = [xbuf[k] for k in range(nc)]
        pf, pb, ff, fl, ll, wf, wl = ([g[:, q : q + 1] for g in got] for q in range(7))
        weights = [half_coupling * jnp.sqrt(wl[k] * wf[k + 1]) for k in range(nc - 1)]
        system = flux_system(weights, ff, fl, ll)
        (fluxes,) = reduce_fluxes(
            *system, [[weights[k] * (pb[k] - pf[k + 1]) for k in range(nc - 1)]]
        )
        zero = jnp.zeros_like(fluxes[0])
        fluxes = [zero] + fluxes + [zero]
        first = [pf[k] + ff[k] * fluxes[k] - fl[k] * fluxes[k + 1] for k in range(nc)] + [zero]
        last = [zero] + [pb[k] + fl[k] * fluxes[k] - ll[k] * fluxes[k + 1] for k in range(nc)]
        entering, leaving, left_of, right_of = zero, zero, zero, zero
        for k in range(nc):
            here = col_at == k
            entering = jnp.where(here, fluxes[k], entering)
            leaving = jnp.where(here, fluxes[k + 1], leaving)
            left_of = jnp.where(here, last[k], left_of)
            right_of = jnp.where(here, first[k + 1], right_of)
        half_step = solved + from_left * entering - from_right * leaving

    loads[4].wait()
    courant = current[...]
    forward = jnp.where(lane == width - 1, right_of, rolled(half_step, -1, 1))
    backward = jnp.where(lane == 0, left_of, rolled(half_step, 1, 1))
    advected = 0.5 * courant * (forward - backward) - 0.5 * courant * courant * (
        forward - 2.0 * half_step + backward
    )
    second_rhs = (1.0 - damping) * half_step - advected

    for q, response in enumerate((from_first, from_last)):
        line = jnp.sum(response * second_rhs, axis=0, keepdims=True)
        for c in range(chunks):
            pbuf[row_at, q, c : c + 1, :] = line[:, c * LANES : (c + 1) * LANES]
    send_rows(pbuf, p_send, p_recv)

    solved_y = solve_y(second_rhs)

    wait_rows(kbuf, k_recv)
    ff, fl, ll, wf, wl = ([kbuf[k, q] for k in range(nr)] for q in range(5))
    weights = [half_coupling * jnp.sqrt(wl[k] * wf[k + 1]) for k in range(nr - 1)]
    system = flux_system(weights, ff, fl, ll)
    rights = [
        [jnp.where(row_at + shift == k, weights[k], 0.0) for k in range(nr - 1)]
        for shift in (-1, 0)
    ]
    into, outof = reduce_fluxes(*system, rights)

    for copy in x_copies:
        copy.wait_send()
    wait_rows(kbuf, k_send)
    wait_rows(pbuf, p_send)
    wait_rows(pbuf, p_recv)
    entering = leaving = jnp.zeros((chunks, LANES), jnp.float32)
    for k in range(nr - 1):
        jump = pbuf[k, 1] - pbuf[k + 1, 0]
        entering = entering + into[k] * jump
        leaving = leaving + outof[k] * jump
    for c in range(chunks):
        at = slice(c * LANES, (c + 1) * LANES)
        out[:, at] = (
            solved_y[:, at]
            + from_first[:, at] * entering[c : c + 1, :]
            - from_last[:, at] * leaving[c : c + 1, :]
        )


def on_device(elevation, water_depth, friction, current_x, wet_mask):
    nr, nc = lax.axis_size("rows"), lax.axis_size("cols")
    height, width = elevation.shape
    chunks = width // LANES
    return pl.pallas_call(
        functools.partial(step_kernel, nr, nc),
        out_shape=jax.ShapeDtypeStruct(elevation.shape, jnp.float32),
        in_specs=[pl.BlockSpec(memory_space=pl.ANY)] * 5,
        out_specs=pl.BlockSpec(memory_space=pltpu.VMEM),
        scratch_shapes=[pltpu.VMEM(elevation.shape, jnp.float32)] * 4
        + [
            pltpu.VMEM(elevation.shape, jnp.int32),
            pltpu.SemaphoreType.DMA((5,)),
            pltpu.VMEM((nc, height, LANES), jnp.float32),
            pltpu.VMEM((nr, 5, chunks, LANES), jnp.float32),
            pltpu.VMEM((nr, 2, chunks, LANES), jnp.float32),
            pltpu.SemaphoreType.DMA((nc - 1,)),
            pltpu.SemaphoreType.DMA((nc - 1,)),
            pltpu.SemaphoreType.DMA,
            pltpu.SemaphoreType.DMA,
            pltpu.SemaphoreType.DMA,
            pltpu.SemaphoreType.DMA,
        ],
        compiler_params=pltpu.CompilerParams(
            collective_id=0, has_side_effects=True, vmem_limit_bytes=55150 * 1024
        ),
    )(elevation, water_depth, friction, current_x, wet_mask)


def solution(mesh):
    placed = P("rows", "cols")
    return jax.shard_map(
        on_device, mesh=mesh, in_specs=(placed,) * 5, out_specs=placed, check_vma=False
    )
```

```python
import functools

import jax
import jax.numpy as jnp
from jax import lax
from jax.experimental import pallas as pl
from jax.experimental.pallas import tpu as pltpu
from jax.sharding import PartitionSpec as P

half_coupling = 50.0
LANES = 128


def rolled(values, shift, axis):
    return pltpu.roll(values, shift % values.shape[axis], axis)


def reduce_lines(face, excess, rights, axis):
    length = face.shape[axis]
    before = rolled(face, 1, axis)
    stride = 1
    steps = []

    def advance(right, to_next, to_prev, stride):
        return (
            right
            + rolled(to_next * right, stride, axis)
            + rolled(to_prev * right, -stride, axis)
        )

    while stride < length:
        inverse = 1.0 / (excess + before + face)
        to_next = face * inverse
        to_prev = before * inverse
        through = to_next * before
        excess = advance(excess, to_next, to_prev, stride)
        rights = [advance(right, to_next, to_prev, stride) for right in rights]
        steps.append((to_next, to_prev, stride))
        face = rolled(through, -stride, axis)
        before = rolled(through, stride, axis)
        stride *= 2
    inverse = 1.0 / excess

    def solve(right):
        for step in steps:
            right = advance(right, *step)
        return right * inverse

    return [right * inverse for right in rights], solve


def reduce_fluxes(lower, middle, upper, rights):
    count = len(middle)
    stride = 1
    while stride < count:
        inverse = [1.0 / m for m in middle]
        new_lower, new_middle, new_upper = [], [], []
        new_rights = [[] for _ in rights]
        for k in range(count):
            a, c, m = None, None, middle[k]
            sums = [right[k] for right in rights]
            if k - stride >= 0:
                w = lower[k] * inverse[k - stride]
                if k - 2 * stride >= 0:
                    a = w * lower[k - stride]
                m = m - w * upper[k - stride]
                sums = [s + w * right[k - stride] for s, right in zip(sums, rights)]
            if k + stride < count:
                w = upper[k] * inverse[k + stride]
                if k + 2 * stride < count:
                    c = w * upper[k + stride]
                m = m - w * lower[k + stride]
                sums = [s + w * right[k + stride] for s, right in zip(sums, rights)]
            new_lower.append(a)
            new_middle.append(m)
            new_upper.append(c)
            for out, s in zip(new_rights, sums):
                out.append(s)
        lower, middle, upper, rights = new_lower, new_middle, new_upper, new_rights
        stride *= 2
    inverse = [1.0 / m for m in middle]
    return [[s * i for s, i in zip(right, inverse)] for right in rights]


def flux_system(weights, first_first, last_first, last_last):
    count = len(weights)
    lower = [weights[k] * last_first[k] for k in range(count)]
    upper = [weights[k] * last_first[k + 1] for k in range(count)]
    middle = [1.0 + weights[k] * (last_last[k] + first_first[k + 1]) for k in range(count)]
    return lower, middle, upper


def step_kernel(
    nr, nc, elevation_hbm, depth_hbm, friction_hbm, current_hbm, mask_hbm, out,
    elevation, depth, friction, current, mask, in_sem,
    xbuf, kbuf, pbuf, x_send, x_recv, k_send, k_recv, p_send, p_recv,
):
    row_at, col_at = lax.axis_index("rows"), lax.axis_index("cols")
    height, width = out.shape
    chunks = width // LANES

    def row_peer(offset):
        return (lax.rem(row_at + offset, nr), col_at)

    def col_peer(offset):
        return (row_at, lax.rem(col_at + offset, nc))

    def send_rows(buffer, send, recv):
        for k in range(nr - 1):
            peer = jnp.where(k >= row_at, k + 1, k)
            pltpu.make_async_remote_copy(
                src_ref=buffer.at[row_at], dst_ref=buffer.at[row_at],
                send_sem=send, recv_sem=recv,
                device_id=(peer, col_at), device_id_type=pl.DeviceIdType.MESH,
            ).start()

    def wait_rows(buffer, semaphore):
        part = buffer.at[pl.ds(0, nr - 1)]
        pltpu.make_async_copy(part, part, semaphore).wait()

    arrays = (
        (depth_hbm, depth), (mask_hbm, mask), (friction_hbm, friction),
        (elevation_hbm, elevation), (current_hbm, current),
    )
    loads = [
        pltpu.make_async_copy(src, dst, in_sem.at[i]) for i, (src, dst) in enumerate(arrays)
    ]
    for load in loads:
        load.start()

    barrier = pltpu.get_barrier_semaphore()
    for k in range(1, nr):
        pl.semaphore_signal(barrier, inc=1, device_id=row_peer(k), device_id_type=pl.DeviceIdType.MESH)
    for k in range(1, nc):
        pl.semaphore_signal(barrier, inc=1, device_id=col_peer(k), device_id_type=pl.DeviceIdType.MESH)

    for load in loads[:3]:
        load.wait()
    still = depth[...]
    wet = still * mask[...].astype(jnp.float32)
    damping = friction[...] / (4.0 * still)
    excess = 1.0 + damping
    lane = lax.broadcasted_iota(jnp.int32, (height, width), 1)
    row = lax.broadcasted_iota(jnp.int32, (height, width), 0)

    face_x = half_coupling * jnp.sqrt(wet * rolled(wet, -1, 1))
    face_x = jnp.where(lane == width - 1, 0.0, face_x)
    loads[3].wait()
    first_rhs = (1.0 - damping) * elevation[...]
    small = lax.broadcasted_iota(jnp.int32, (height, LANES), 1)
    at_left = col_at == 0
    if nc == 2:
        edge = jnp.where(at_left, width - 1, 0)
        unit = jnp.where(lane == edge, 1.0, 0.0)
        (spike, solved), _ = reduce_lines(face_x, excess, [unit, first_rhs], 1)
        message = None
        for q, values in enumerate((solved, spike, wet)):
            chunk = jnp.where(at_left, values[:, width - LANES :], values[:, :LANES])
            chunk = pltpu.roll(chunk, q + jnp.where(at_left, 1, 0), 1)
            message = chunk if q == 0 else jnp.where(small == q, chunk, message)
    else:
        units = [jnp.where(lane == 0, 1.0, 0.0), jnp.where(lane == width - 1, 1.0, 0.0)]
        (from_left, from_right), solve_x = reduce_lines(face_x, excess, units, 1)
        solved = solve_x(first_rhs)
        message = jnp.zeros((height, LANES), jnp.float32)
        columns = (
            solved[:, 0:1], solved[:, width - 1 : width], from_left[:, 0:1],
            from_left[:, width - 1 : width], from_right[:, width - 1 : width],
            wet[:, 0:1], wet[:, width - 1 : width],
        )
        for q, column in enumerate(columns):
            message = jnp.where(small == q, column, message)
    xbuf[col_at] = message
    x_copies = [
        pltpu.make_async_remote_copy(
            src_ref=xbuf.at[col_at], dst_ref=xbuf.at[col_at],
            send_sem=x_send.at[k - 1], recv_sem=x_recv.at[k - 1],
            device_id=col_peer(k), device_id_type=pl.DeviceIdType.MESH,
        )
        for k in range(1, nc)
    ]
    pl.semaphore_wait(barrier, nr + nc - 2)
    for copy in x_copies:
        copy.start()

    face = half_coupling * jnp.sqrt(wet * rolled(wet, -1, 0))
    face = jnp.where(row == height - 1, 0.0, face)
    unit_first = jnp.where(row == 0, 1.0, 0.0)
    unit_last = jnp.where(row == height - 1, 1.0, 0.0)
    (from_first, from_last), solve_y = reduce_lines(face, excess, [unit_first, unit_last], 0)
    ends = (
        from_first[0:1], from_first[height - 1 : height], from_last[height - 1 : height],
        wet[0:1], wet[height - 1 : height],
    )
    for q, line in enumerate(ends):
        for c in range(chunks):
            kbuf[row_at, q, c : c + 1, :] = line[:, c * LANES : (c + 1) * LANES]
    send_rows(kbuf, k_send, k_recv)
    for copy in x_copies:
        copy.wait_recv()

    if nc == 2:
        other = xbuf[1 - col_at]
        p, s, w = (message[:, q : q + 1] for q in range(3))
        other_p, other_s, other_w = (other[:, q : q + 1] for q in range(3))
        weight = half_coupling * jnp.sqrt(w * other_w)
        flux = weight * (p - other_p) / (1.0 + weight * (s + other_s))
        half_step = solved - spike * flux
        beyond = other_p + other_s * flux
        right_of = jnp.where(at_left, beyond, 0.0)
        left_of = jnp.where(at_left, 0.0, beyond)
    else:
        got = [xbuf[k] for k in range(nc)]
        pf, pb, ff, fl, ll, wf, wl = ([g[:, q : q + 1] for g in got] for q in range(7))
        weights = [half_coupling * jnp.sqrt(wl[k] * wf[k + 1]) for k in range(nc - 1)]
        system = flux_system(weights, ff, fl, ll)
        (fluxes,) = reduce_fluxes(
            *system, [[weights[k] * (pb[k] - pf[k + 1]) for k in range(nc - 1)]]
        )
        zero = jnp.zeros_like(fluxes[0])
        fluxes = [zero] + fluxes + [zero]
        first = [pf[k] + ff[k] * fluxes[k] - fl[k] * fluxes[k + 1] for k in range(nc)] + [zero]
        last = [zero] + [pb[k] + fl[k] * fluxes[k] - ll[k] * fluxes[k + 1] for k in range(nc)]
        entering, leaving, left_of, right_of = zero, zero, zero, zero
        for k in range(nc):
            here = col_at == k
            entering = jnp.where(here, fluxes[k], entering)
            leaving = jnp.where(here, fluxes[k + 1], leaving)
            left_of = jnp.where(here, last[k], left_of)
            right_of = jnp.where(here, first[k + 1], right_of)
        half_step = solved + from_left * entering - from_right * leaving

    loads[4].wait()
    courant = current[...]
    forward = jnp.where(lane == width - 1, right_of, rolled(half_step, -1, 1))
    backward = jnp.where(lane == 0, left_of, rolled(half_step, 1, 1))
    advected = 0.5 * courant * (forward - backward) - 0.5 * courant * courant * (
        forward - 2.0 * half_step + backward
    )
    second_rhs = (1.0 - damping) * half_step - advected

    for q, response in enumerate((from_first, from_last)):
        line = jnp.sum(response * second_rhs, axis=0, keepdims=True)
        for c in range(chunks):
            pbuf[row_at, q, c : c + 1, :] = line[:, c * LANES : (c + 1) * LANES]
    send_rows(pbuf, p_send, p_recv)

    solved_y = solve_y(second_rhs)

    wait_rows(kbuf, k_recv)
    ff, fl, ll, wf, wl = ([kbuf[k, q] for k in range(nr)] for q in range(5))
    weights = [half_coupling * jnp.sqrt(wl[k] * wf[k + 1]) for k in range(nr - 1)]
    system = flux_system(weights, ff, fl, ll)
    rights = [
        [jnp.where(row_at + shift == k, weights[k], 0.0) for k in range(nr - 1)]
        for shift in (-1, 0)
    ]
    into, outof = reduce_fluxes(*system, rights)

    for copy in x_copies:
        copy.wait_send()
    wait_rows(kbuf, k_send)
    wait_rows(pbuf, p_send)
    wait_rows(pbuf, p_recv)
    entering = leaving = jnp.zeros((chunks, LANES), jnp.float32)
    for k in range(nr - 1):
        jump = pbuf[k, 1] - pbuf[k + 1, 0]
        entering = entering + into[k] * jump
        leaving = leaving + outof[k] * jump
    for c in range(chunks):
        at = slice(c * LANES, (c + 1) * LANES)
        out[:, at] = (
            solved_y[:, at]
            + from_first[:, at] * entering[c : c + 1, :]
            - from_last[:, at] * leaving[c : c + 1, :]
        )


def on_device(elevation, water_depth, friction, current_x, wet_mask):
    nr, nc = lax.axis_size("rows"), lax.axis_size("cols")
    height, width = elevation.shape
    chunks = width // LANES
    return pl.pallas_call(
        functools.partial(step_kernel, nr, nc),
        out_shape=jax.ShapeDtypeStruct(elevation.shape, jnp.float32),
        in_specs=[pl.BlockSpec(memory_space=pl.ANY)] * 5,
        out_specs=pl.BlockSpec(memory_space=pltpu.VMEM),
        scratch_shapes=[pltpu.VMEM(elevation.shape, jnp.float32)] * 4
        + [
            pltpu.VMEM(elevation.shape, jnp.int32),
            pltpu.SemaphoreType.DMA((5,)),
            pltpu.VMEM((nc, height, LANES), jnp.float32),
            pltpu.VMEM((nr, 5, chunks, LANES), jnp.float32),
            pltpu.VMEM((nr, 2, chunks, LANES), jnp.float32),
            pltpu.SemaphoreType.DMA((nc - 1,)),
            pltpu.SemaphoreType.DMA((nc - 1,)),
            pltpu.SemaphoreType.DMA,
            pltpu.SemaphoreType.DMA,
            pltpu.SemaphoreType.DMA,
            pltpu.SemaphoreType.DMA,
        ],
        compiler_params=pltpu.CompilerParams(
            collective_id=0, has_side_effects=True, vmem_limit_bytes=55150 * 1024
        ),
    )(elevation, water_depth, friction, current_x, wet_mask)


def solution(mesh):
    placed = P("rows", "cols")
    return jax.shard_map(
        on_device, mesh=mesh, in_specs=(placed,) * 5, out_specs=placed, check_vma=False
    )
```

```python
import functools

import jax
import jax.numpy as jnp
from jax import lax
from jax.experimental import pallas as pl
from jax.experimental.pallas import tpu as pltpu
from jax.sharding import PartitionSpec as P

half_coupling = 50.0
LANES = 128


def rolled(values, shift, axis):
    return pltpu.roll(values, shift % values.shape[axis], axis)


def reduce_lines(face, excess, rights, axis):
    length = face.shape[axis]
    before = rolled(face, 1, axis)
    stride = 1
    steps = []

    def advance(right, to_next, to_prev, stride):
        return (
            right
            + rolled(to_next * right, stride, axis)
            + rolled(to_prev * right, -stride, axis)
        )

    while stride < length:
        inverse = 1.0 / (excess + before + face)
        to_next = face * inverse
        to_prev = before * inverse
        through = to_next * before
        excess = advance(excess, to_next, to_prev, stride)
        rights = [advance(right, to_next, to_prev, stride) for right in rights]
        steps.append((to_next, to_prev, stride))
        face = rolled(through, -stride, axis)
        before = rolled(through, stride, axis)
        stride *= 2
    inverse = 1.0 / excess

    def solve(right):
        for step in steps:
            right = advance(right, *step)
        return right * inverse

    return [right * inverse for right in rights], solve


def reduce_fluxes(lower, middle, upper, rights):
    count = len(middle)
    stride = 1
    while stride < count:
        inverse = [1.0 / m for m in middle]
        new_lower, new_middle, new_upper = [], [], []
        new_rights = [[] for _ in rights]
        for k in range(count):
            a, c, m = None, None, middle[k]
            sums = [right[k] for right in rights]
            if k - stride >= 0:
                w = lower[k] * inverse[k - stride]
                if k - 2 * stride >= 0:
                    a = w * lower[k - stride]
                m = m - w * upper[k - stride]
                sums = [s + w * right[k - stride] for s, right in zip(sums, rights)]
            if k + stride < count:
                w = upper[k] * inverse[k + stride]
                if k + 2 * stride < count:
                    c = w * upper[k + stride]
                m = m - w * lower[k + stride]
                sums = [s + w * right[k + stride] for s, right in zip(sums, rights)]
            new_lower.append(a)
            new_middle.append(m)
            new_upper.append(c)
            for out, s in zip(new_rights, sums):
                out.append(s)
        lower, middle, upper, rights = new_lower, new_middle, new_upper, new_rights
        stride *= 2
    inverse = [1.0 / m for m in middle]
    return [[s * i for s, i in zip(right, inverse)] for right in rights]


def flux_system(weights, first_first, last_first, last_last):
    count = len(weights)
    lower = [weights[k] * last_first[k] for k in range(count)]
    upper = [weights[k] * last_first[k + 1] for k in range(count)]
    middle = [1.0 + weights[k] * (last_last[k] + first_first[k + 1]) for k in range(count)]
    return lower, middle, upper


def step_kernel(
    nr, nc, elevation_hbm, depth_hbm, friction_hbm, current_hbm, mask_hbm, out,
    elevation, depth, friction, current, mask, in_sem,
    xbuf, kbuf, pbuf, x_send, x_recv, k_send, k_recv, p_send, p_recv,
):
    row_at, col_at = lax.axis_index("rows"), lax.axis_index("cols")
    height, width = out.shape
    chunks = width // LANES

    def row_peer(offset):
        return (lax.rem(row_at + offset, nr), col_at)

    def col_peer(offset):
        return (row_at, lax.rem(col_at + offset, nc))

    def send_rows(buffer, send, recv):
        for k in range(nr - 1):
            peer = jnp.where(k >= row_at, k + 1, k)
            pltpu.make_async_remote_copy(
                src_ref=buffer.at[row_at], dst_ref=buffer.at[row_at],
                send_sem=send, recv_sem=recv,
                device_id=(peer, col_at), device_id_type=pl.DeviceIdType.MESH,
            ).start()

    def wait_rows(buffer, semaphore):
        part = buffer.at[pl.ds(0, nr - 1)]
        pltpu.make_async_copy(part, part, semaphore).wait()

    arrays = (
        (depth_hbm, depth), (mask_hbm, mask), (friction_hbm, friction),
        (elevation_hbm, elevation), (current_hbm, current),
    )
    loads = [
        pltpu.make_async_copy(src, dst, in_sem.at[i]) for i, (src, dst) in enumerate(arrays)
    ]
    for load in loads:
        load.start()

    barrier = pltpu.get_barrier_semaphore()
    for k in range(1, nr):
        pl.semaphore_signal(barrier, inc=1, device_id=row_peer(k), device_id_type=pl.DeviceIdType.MESH)
    for k in range(1, nc):
        pl.semaphore_signal(barrier, inc=1, device_id=col_peer(k), device_id_type=pl.DeviceIdType.MESH)

    for load in loads[:3]:
        load.wait()
    still = depth[...]
    wet = still * mask[...].astype(jnp.float32)
    damping = friction[...] / (4.0 * still)
    excess = 1.0 + damping
    lane = lax.broadcasted_iota(jnp.int32, (height, width), 1)
    row = lax.broadcasted_iota(jnp.int32, (height, width), 0)

    face_x = half_coupling * jnp.sqrt(wet * rolled(wet, -1, 1))
    face_x = jnp.where(lane == width - 1, 0.0, face_x)
    loads[3].wait()
    first_rhs = (1.0 - damping) * elevation[...]
    small = lax.broadcasted_iota(jnp.int32, (height, LANES), 1)
    at_left = col_at == 0
    if nc == 2:
        edge = jnp.where(at_left, width - 1, 0)
        unit = jnp.where(lane == edge, 1.0, 0.0)
        (spike, solved), _ = reduce_lines(face_x, excess, [unit, first_rhs], 1)
        message = None
        for q, values in enumerate((solved, spike, wet)):
            chunk = jnp.where(at_left, values[:, width - LANES :], values[:, :LANES])
            chunk = pltpu.roll(chunk, q + jnp.where(at_left, 1, 0), 1)
            message = chunk if q == 0 else jnp.where(small == q, chunk, message)
    else:
        units = [jnp.where(lane == 0, 1.0, 0.0), jnp.where(lane == width - 1, 1.0, 0.0)]
        (from_left, from_right), solve_x = reduce_lines(face_x, excess, units, 1)
        solved = solve_x(first_rhs)
        message = jnp.zeros((height, LANES), jnp.float32)
        columns = (
            solved[:, 0:1], solved[:, width - 1 : width], from_left[:, 0:1],
            from_left[:, width - 1 : width], from_right[:, width - 1 : width],
            wet[:, 0:1], wet[:, width - 1 : width],
        )
        for q, column in enumerate(columns):
            message = jnp.where(small == q, column, message)
    xbuf[col_at] = message
    x_copies = [
        pltpu.make_async_remote_copy(
            src_ref=xbuf.at[col_at], dst_ref=xbuf.at[col_at],
            send_sem=x_send.at[k - 1], recv_sem=x_recv.at[k - 1],
            device_id=col_peer(k), device_id_type=pl.DeviceIdType.MESH,
        )
        for k in range(1, nc)
    ]
    pl.semaphore_wait(barrier, nr + nc - 2)
    for copy in x_copies:
        copy.start()

    face = half_coupling * jnp.sqrt(wet * rolled(wet, -1, 0))
    face = jnp.where(row == height - 1, 0.0, face)
    unit_first = jnp.where(row == 0, 1.0, 0.0)
    unit_last = jnp.where(row == height - 1, 1.0, 0.0)
    (from_first, from_last), solve_y = reduce_lines(face, excess, [unit_first, unit_last], 0)
    ends = (
        from_first[0:1], from_first[height - 1 : height], from_last[height - 1 : height],
        wet[0:1], wet[height - 1 : height],
    )
    for q, line in enumerate(ends):
        for c in range(chunks):
            kbuf[row_at, q, c : c + 1, :] = line[:, c * LANES : (c + 1) * LANES]
    send_rows(kbuf, k_send, k_recv)
    loads[4].wait()
    half_courant = 0.5 * current[...]
    half_square = half_courant * current[...]
    ahead, behind = half_square - half_courant, half_square + half_courant
    centre = (1.0 - damping) - 2.0 * half_square

    for copy in x_copies:
        copy.wait_recv()

    if nc == 2:
        other = xbuf[1 - col_at]
        p, s, w = (message[:, q : q + 1] for q in range(3))
        other_p, other_s, other_w = (other[:, q : q + 1] for q in range(3))
        weight = half_coupling * jnp.sqrt(w * other_w)
        flux = weight * (p - other_p) / (1.0 + weight * (s + other_s))
        half_step = solved - spike * flux
        beyond = other_p + other_s * flux
        right_of = jnp.where(at_left, beyond, 0.0)
        left_of = jnp.where(at_left, 0.0, beyond)
    else:
        got = [xbuf[k] for k in range(nc)]
        pf, pb, ff, fl, ll, wf, wl = ([g[:, q : q + 1] for g in got] for q in range(7))
        weights = [half_coupling * jnp.sqrt(wl[k] * wf[k + 1]) for k in range(nc - 1)]
        system = flux_system(weights, ff, fl, ll)
        (fluxes,) = reduce_fluxes(
            *system, [[weights[k] * (pb[k] - pf[k + 1]) for k in range(nc - 1)]]
        )
        zero = jnp.zeros_like(fluxes[0])
        fluxes = [zero] + fluxes + [zero]
        first = [pf[k] + ff[k] * fluxes[k] - fl[k] * fluxes[k + 1] for k in range(nc)] + [zero]
        last = [zero] + [pb[k] + fl[k] * fluxes[k] - ll[k] * fluxes[k + 1] for k in range(nc)]
        entering, leaving, left_of, right_of = zero, zero, zero, zero
        for k in range(nc):
            here = col_at == k
            entering = jnp.where(here, fluxes[k], entering)
            leaving = jnp.where(here, fluxes[k + 1], leaving)
            left_of = jnp.where(here, last[k], left_of)
            right_of = jnp.where(here, first[k + 1], right_of)
        half_step = solved + from_left * entering - from_right * leaving

    forward = jnp.where(lane == width - 1, right_of, rolled(half_step, -1, 1))
    backward = jnp.where(lane == 0, left_of, rolled(half_step, 1, 1))
    second_rhs = centre * half_step + ahead * forward + behind * backward

    for q, response in enumerate((from_first, from_last)):
        line = jnp.sum(response * second_rhs, axis=0, keepdims=True)
        for c in range(chunks):
            pbuf[row_at, q, c : c + 1, :] = line[:, c * LANES : (c + 1) * LANES]
    send_rows(pbuf, p_send, p_recv)

    solved_y = solve_y(second_rhs)

    wait_rows(kbuf, k_recv)
    ff, fl, ll, wf, wl = ([kbuf[k, q] for k in range(nr)] for q in range(5))
    weights = [half_coupling * jnp.sqrt(wl[k] * wf[k + 1]) for k in range(nr - 1)]
    system = flux_system(weights, ff, fl, ll)
    rights = [
        [jnp.where(row_at + shift == k, weights[k], 0.0) for k in range(nr - 1)]
        for shift in (-1, 0)
    ]
    into, outof = reduce_fluxes(*system, rights)

    for copy in x_copies:
        copy.wait_send()
    wait_rows(kbuf, k_send)
    wait_rows(pbuf, p_send)
    wait_rows(pbuf, p_recv)
    entering = leaving = jnp.zeros((chunks, LANES), jnp.float32)
    for k in range(nr - 1):
        jump = pbuf[k, 1] - pbuf[k + 1, 0]
        entering = entering + into[k] * jump
        leaving = leaving + outof[k] * jump
    for c in range(chunks):
        at = slice(c * LANES, (c + 1) * LANES)
        out[:, at] = (
            solved_y[:, at]
            + from_first[:, at] * entering[c : c + 1, :]
            - from_last[:, at] * leaving[c : c + 1, :]
        )


def on_device(elevation, water_depth, friction, current_x, wet_mask):
    nr, nc = lax.axis_size("rows"), lax.axis_size("cols")
    height, width = elevation.shape
    chunks = width // LANES
    return pl.pallas_call(
        functools.partial(step_kernel, nr, nc),
        out_shape=jax.ShapeDtypeStruct(elevation.shape, jnp.float32),
        in_specs=[pl.BlockSpec(memory_space=pl.ANY)] * 5,
        out_specs=pl.BlockSpec(memory_space=pltpu.VMEM),
        scratch_shapes=[pltpu.VMEM(elevation.shape, jnp.float32)] * 4
        + [
            pltpu.VMEM(elevation.shape, jnp.int32),
            pltpu.SemaphoreType.DMA((5,)),
            pltpu.VMEM((nc, height, LANES), jnp.float32),
            pltpu.VMEM((nr, 5, chunks, LANES), jnp.float32),
            pltpu.VMEM((nr, 2, chunks, LANES), jnp.float32),
            pltpu.SemaphoreType.DMA((nc - 1,)),
            pltpu.SemaphoreType.DMA((nc - 1,)),
            pltpu.SemaphoreType.DMA,
            pltpu.SemaphoreType.DMA,
            pltpu.SemaphoreType.DMA,
            pltpu.SemaphoreType.DMA,
        ],
        compiler_params=pltpu.CompilerParams(
            collective_id=0, has_side_effects=True, vmem_limit_bytes=55150 * 1024
        ),
    )(elevation, water_depth, friction, current_x, wet_mask)


def solution(mesh):
    placed = P("rows", "cols")
    return jax.shard_map(
        on_device, mesh=mesh, in_specs=(placed,) * 5, out_specs=placed, check_vma=False
    )
```
